256 devices in a mesh: section: 32 (over y_hi, z, core), tp: 8 (over x, y_lo).
Axes of the slice: x: 4, y: 4 (y_hi: 2, y_lo: 2; y = y_hi * 2 + y_lo), z: 8, core: 2. Of those that a mesh axis runs over, the one named last changes fastest.
Arguments:
- acts_in: bfloat16 [2, 32, 128, 6144], P(None, 'section', None, 'tp'), may hold values from -6 to 6
- cots_in: bfloat16 [2, 32, 128, 6144], P(None, 'section', None, 'tp'), may hold values from -8 to 8
- stash: bfloat16 [2, 2, 32, 128, 6144], P(None, None, 'section', None, 'tp'), may hold values from -8 to 8
- fresh_acts: bfloat16 [2, 1, 128, 6144], P(None, None, None, 'tp'), may hold values from -6 to 6
- fresh_cots: bfloat16 [2, 1, 128, 6144], P(None, None, None, 'tp'), may hold values from -8 to 8
- gains: bfloat16 [32, 6144], P('section'), may hold values from 0.5 to 1.5
- weights: bfloat16 [32, 6144, 6144], P('section', None, 'tp'), may hold values from -1.5 to 2
- adapter_a: bfloat16 [32, 8, 6144], P('section'), may hold values from -0.078125 to 0.078125
- adapter_b: bfloat16 [32, 8, 6144], P('section', None, 'tp'), may hold values from -2 to 2
Outputs:
- acts_out: bfloat16 [2, 2, 32, 128, 6144], P(None, None, 'section', None, 'tp')
- input_grads: bfloat16 [2, 2, 32, 128, 6144], P(None, None, 'section', None, 'tp')
- grad_a: bfloat16 [32, 8, 6144], P('section')
- grad_b: bfloat16 [32, 8, 6144], P('section', None, 'tp')
The draws below stay inside these ranges and needn't reach their ends.
All inputs are finite; a program needn't handle non-finite values.
Results may differ from the reference program's by a relative error of at most 0.019.
Values may be sent and summed in bfloat16 or wider, within the bound.
A program may use at most 128 MiB of HBM per device.

```python
import math
import jax
import jax.numpy as jnp
from jax import lax

D = 6144
RANK = 8
ROWS = 128
TICKS = 2
SECTIONS = 32
N_TP = 8


def shared_part(key, amp_lo, amp_hi):
    key_dir, key_scale, key_group, key_amp = jax.random.split(key, 4)
    direction = jax.random.normal(key_dir, (D,), jnp.float32)
    scales = jnp.exp(jax.random.uniform(key_scale, (D,), jnp.float32, math.log(0.3), math.log(3.0)))
    pattern = direction * scales
    groups = jax.random.uniform(key_group, (32,), jnp.float32, -0.5, 1.5)
    owner = jnp.arange(D) * 32 // D
    picks = (owner[:, None] == jnp.arange(32)[None, :]).astype(jnp.float32)
    region = jnp.sum(picks * groups[None, :], axis=1)
    amplitude = jnp.exp(jax.random.uniform(key_amp, (ROWS,), jnp.float32, math.log(amp_lo), math.log(amp_hi)))
    return (amplitude[:, None] * pattern[None, :], amplitude[:, None] * (pattern * region)[None, :])


def noisy(key, shape, shared):
    noise = jax.random.normal(key, shape, jnp.float32)
    return jnp.clip(noise + shared, -8.0, 8.0)


def pick_shared(key):
    return shared_part(key, 0.7, 1.4)


def draw_stash(key, part):
    row_part, cot_part = pick_shared(key)
    key = jax.random.fold_in(key, 11)
    return noisy(key, (2, TICKS, SECTIONS, ROWS, D), row_part).astype(jnp.bfloat16)


def draw_cots_in(key, part):
    row_part, cot_part = pick_shared(key)
    key = jax.random.fold_in(key, 12)
    return noisy(key, (2, SECTIONS, ROWS, D), cot_part).astype(jnp.bfloat16)


def draw_fresh_cots(key, part):
    row_part, cot_part = pick_shared(key)
    key = jax.random.fold_in(key, 13)
    return noisy(key, (2, TICKS - 1, ROWS, D), cot_part).astype(jnp.bfloat16)


def draw_weights(key, part):
    key = jax.random.fold_in(key, 14)
    key_noise, key_diag = jax.random.split(key)
    spread = 1.0 / math.sqrt(D)
    noise = jnp.clip(jax.random.normal(key_noise, (SECTIONS, D, D), jnp.float32), -6.0, 6.0) * spread
    diagonal = jax.random.uniform(key_diag, (SECTIONS, D), jnp.float32, 0.7, 1.3)
    same = (jnp.arange(D)[:, None] == jnp.arange(D)[None, :]).astype(jnp.float32)
    return (noise + same[None, :, :] * diagonal[:, :, None]).astype(jnp.bfloat16)


def shard_levels(rng, dims, pieces, low, high):
    loudness = 1.0
    for position, parts in pieces:
        heights = jax.random.uniform(jax.random.fold_in(jax.random.fold_in(rng, 6), position), (parts,), jnp.float32, low / len(pieces), high / len(pieces))
        loudness = loudness * jnp.repeat(jnp.exp(heights), dims[position] // parts).reshape((-1,) + (1,) * (len(dims) - 1 - position))
    return loudness


def centred(key, shape, deviation, bound, cuts=(), dtype=jnp.bfloat16):
    values = jax.random.normal(key, shape, jnp.float32) * deviation
    if len(cuts) > 0:
        values = shard_levels(key, shape, cuts, -0.22, 0.18) * values
    return jnp.clip(values, min=-bound, max=bound).astype(dtype)


def setup_inputs(seed: int = 0) -> dict:
    keys = jax.random.split(jax.random.key(seed), 10)
    return {
        "acts_in": centred(keys[0], (2, SECTIONS, ROWS, D), 1.0, 6.0, ((1, 32), (3, 8))),
        "cots_in": draw_cots_in(jax.random.fold_in(keys[9], 71), 0),
        "stash": draw_stash(jax.random.fold_in(keys[9], 71), 0),
        "fresh_acts": centred(keys[3], (2, TICKS - 1, ROWS, D), 1.0, 6.0, ((3, 8),)),
        "fresh_cots": draw_fresh_cots(jax.random.fold_in(keys[9], 71), 0),
        "gains": jnp.clip(1.0 + 0.1 * jax.random.normal(keys[5], (SECTIONS, D), jnp.float32), 0.5, 1.5).astype(jnp.bfloat16),
        "weights": draw_weights(jax.random.fold_in(keys[9], 71), 0),
        "adapter_a": centred(keys[7], (SECTIONS, RANK, D), D ** -0.5, 0.078125, ((0, 32),)),
        "adapter_b": centred(keys[8], (SECTIONS, RANK, D), RANK ** -0.5, 2.0, ((0, 32), (2, 8))),
    }


EPS = 1e-05

def normalize(floats, gain):
    inv_rms = lax.rsqrt(lax.optimization_barrier(jnp.mean(floats * floats, axis=-1, keepdims=True)) + EPS)
    unit = floats * inv_rms
    normed = (unit * gain.astype(jnp.float32)).astype(jnp.bfloat16)
    return (inv_rms, unit, normed)

def section_forward(rows_in, gain, weight, lower, upper):
    floats = rows_in.astype(jnp.float32)
    inv_rms, unit, normed = normalize(floats, gain)
    latent = jnp.dot(normed, lower.T, preferred_element_type=jnp.float32).astype(jnp.bfloat16)
    result = floats + jnp.dot(normed, weight, preferred_element_type=jnp.float32)
    result = result + jnp.dot(latent, upper, preferred_element_type=jnp.float32)
    return result.astype(jnp.bfloat16)

def section_backward(rows_in, cotangent, gain, weight, lower, upper):
    floats = rows_in.astype(jnp.float32)
    inv_rms, unit, normed = normalize(floats, gain)
    latent = jnp.dot(normed, lower.T, preferred_element_type=jnp.float32).astype(jnp.bfloat16)
    width = weight.shape[0]
    block = width // N_TP
    base = jnp.zeros((rows_in.shape[0], width), jnp.float32)
    low_sum = jnp.zeros((rows_in.shape[0], lower.shape[0]), jnp.float32)
    for index in range(N_TP):
        piece = cotangent[:, index * block:(index + 1) * block]
        part = jnp.dot(piece, weight[:, index * block:(index + 1) * block].T, preferred_element_type=jnp.float32)
        base = base + lax.optimization_barrier(part.astype(jnp.bfloat16)).astype(jnp.float32)
        low_part = jnp.dot(piece, upper[:, index * block:(index + 1) * block].T, preferred_element_type=jnp.float32)
        low_sum = low_sum + lax.optimization_barrier(low_part.astype(jnp.bfloat16)).astype(jnp.float32)
    grad_norm = base + jnp.dot(low_sum, lower.astype(jnp.float32), precision=lax.Precision.HIGHEST)
    gain_f = gain.astype(jnp.float32)
    stat = lax.optimization_barrier(jnp.mean(gain_f * unit * grad_norm, axis=-1, keepdims=True))
    back = (cotangent.astype(jnp.float32) + inv_rms * (gain_f * grad_norm - unit * stat)).astype(jnp.bfloat16)
    grad_lower = jnp.dot(low_sum.astype(jnp.bfloat16).T, normed, preferred_element_type=jnp.float32)
    grad_upper = jnp.dot(latent.T, cotangent, preferred_element_type=jnp.float32)
    return (back, grad_lower, grad_upper)

def section_order(array, axis):
    return jnp.stack([array[0], jnp.flip(array[1], axis)])

def reference(acts_in, cots_in, stash, fresh_acts, fresh_cots, gains, weights, adapter_a, adapter_b):
    acts = section_order(acts_in, 0)
    cots = section_order(cots_in, 0)
    kept = section_order(stash, 1)
    width = weights.shape[1]
    micro = acts.shape[2]
    grad_a = jnp.zeros(adapter_a.shape, jnp.float32)
    grad_b = jnp.zeros(adapter_b.shape, jnp.float32)
    outputs = []
    backs = []
    for tick in range(TICKS):

        def forward_one(items):
            pair, gain, weight, lower, upper = items
            result = section_forward(pair.reshape(2 * micro, width), gain, weight, lower, upper)
            return result.reshape(2, micro, width)

        def backward_one(items):
            pair, cot_pair, gain, weight, lower, upper = items
            back, grad_lower, grad_upper = section_backward(pair.reshape(2 * micro, width), cot_pair.reshape(2 * micro, width), gain, weight, lower, upper)
            return (back.reshape(2, micro, width), grad_lower, grad_upper)
        ahead = lax.map(forward_one, (jnp.swapaxes(acts, 0, 1), gains, weights, adapter_a, adapter_b))
        back, grad_lower, grad_upper = lax.map(backward_one, (jnp.swapaxes(kept[:, tick], 0, 1), jnp.swapaxes(cots, 0, 1), gains, weights, adapter_a, adapter_b))
        grad_a = grad_a + grad_lower
        grad_b = grad_b + grad_upper
        ahead = jnp.swapaxes(ahead, 0, 1)
        back = jnp.swapaxes(back, 0, 1)
        outputs.append(ahead)
        backs.append(back)
        if tick + 1 < TICKS:
            acts = jnp.concatenate([fresh_acts[:, tick][:, None], ahead[:, :-1]], axis=1)
            cots = jnp.concatenate([back[:, 1:], fresh_cots[:, tick][:, None]], axis=1)
    acts_out = section_order(jnp.stack(outputs, axis=1), 1)
    input_grads = section_order(jnp.stack(backs, axis=1), 1)
    return (acts_out, input_grads, grad_a.astype(jnp.bfloat16), grad_b.astype(jnp.bfloat16))
```

```python
import jax
import jax.numpy as jnp
from jax import lax
from jax.experimental import pallas as pl
from jax.experimental.pallas import tpu as pltpu
from jax.sharding import PartitionSpec as P

EPS = 1e-05
MESH = pl.DeviceIdType.MESH
F32 = jnp.float32
BF16 = jnp.bfloat16

D0, U0, D1, U1 = range(4)


def contract_last(left, right):
    return lax.dot_general(left, right, (((1,), (1,)), ((), ())), preferred_element_type=F32)


def contract_first(left, right):
    return lax.dot_general(left, right, (((0,), (0,)), ((), ())), preferred_element_type=F32)


def kernel(
    acts, cots, stash, fresh_acts, fresh_cots, gain, weights, lower, upper,
    acts_out, grads_out, grad_a, grad_b,
    w, x, c, s, fa, fc, ps, pr, yb, gb, sm, gar, acc, acc_g, sq, left, right, ga_acc, gb_acc,
    w_sem, in_sem, out_sem,
    ag_s, ag_r, rs_s, rs_r, sm_s, sm_r, sh_s, sh_r, ri_s, ri_r, ro_s, ro_r, ga_s, ga_r,
):
    sec, tp = lax.axis_index("section"), lax.axis_index("tp")
    n_sec, n_tp = lax.axis_size("section"), lax.axis_size("tp")
    cols = w.shape[1]
    width = n_tp * cols
    rank = lower.shape[1]
    nx = n_tp // 2
    xi, yi = tp // 2, tp % 2
    turn = 1 - 2 * yi
    xp, xm, x2 = (xi + turn + nx) % nx, (xi - turn + nx) % nx, (xi + 2) % nx
    yo = 1 - yi
    own, across = tp, xi * 2 + yo
    pp, po, mm, mo, tt, to = xp * 2 + yi, xp * 2 + yo, xm * 2 + yi, xm * 2 + yo, x2 * 2 + yi, x2 * 2 + yo
    ahead, behind, mirror = (sec + 1) % n_sec, (sec + n_sec - 1) % n_sec, n_sec - 1 - sec
    sends = []

    def send(src, dst, send_sem, recv_sem, to_sec, to_tp):
        copy = pltpu.make_async_remote_copy(
            src_ref=src, dst_ref=dst, send_sem=send_sem, recv_sem=recv_sem,
            device_id=(to_sec, to_tp), device_id_type=MESH,
        )
        copy.start()
        sends.append(copy)
        return copy

    def block(index):
        return pl.ds(pl.multiple_of(index * cols, cols), cols)

    order = (tt, to, po, mm, pp, mo, across, own)
    loads = [
        pltpu.make_async_copy(acts.at[0, 0], x.at[D0, own], in_sem.at[0]),
        pltpu.make_async_copy(cots.at[0, 0], c.at[D0], in_sem.at[1]),
    ]
    w_loads = [
        pltpu.make_async_copy(weights.at[0, block(which)], w.at[block(which)], w_sem.at[i])
        for i, which in enumerate(order)
    ]
    loads += [
        pltpu.make_async_copy(stash.at[0, 0, 0], s.at[D0], in_sem.at[2]),
        pltpu.make_async_copy(stash.at[0, 1, 0], s.at[D1], in_sem.at[3]),
        pltpu.make_async_copy(fresh_acts.at[:, 0], fa, in_sem.at[4]),
        pltpu.make_async_copy(fresh_cots.at[:, 0], fc, in_sem.at[5]),
    ]
    for copy in loads[:2] + w_loads + loads[2:]:
        copy.start()

    barrier = pltpu.get_barrier_semaphore()
    peers = [(sec, (tp + k) % n_tp) for k in range(1, n_tp)]
    peers += [(mirror, tp), (ahead, tp), (behind, tp)]
    for peer in peers:
        pl.semaphore_signal(barrier, inc=1, device_id=peer, device_id_type=MESH)
    pl.semaphore_wait(barrier, len(peers))

    rev_c = send(cots.at[1, 0], c.at[U0], ri_s.at[0], ri_r.at[0], mirror, tp)
    rev_x = send(acts.at[1, 0], x.at[U0, own], ri_s.at[1], ri_r.at[1], mirror, tp)
    rev_s = {
        U0: send(stash.at[1, 0, 0], s.at[U0], ri_s.at[2], ri_r.at[2], mirror, tp),
        U1: send(stash.at[1, 1, 0], s.at[U1], ri_s.at[3], ri_r.at[3], mirror, tp),
    }

    left[0:rank] = lower[0].astype(F32)
    left[rank:2 * rank] = jnp.broadcast_to(gain[...].astype(F32), (rank, width))
    row = lax.broadcasted_iota(jnp.int32, (rank, 128), 0)
    right[0:rank, 0:cols] = upper[0].astype(F32)
    right[rank:2 * rank, 0:cols] = jnp.zeros((rank, cols), F32)
    right[0:rank, cols:cols + 128] = jnp.zeros((rank, 128), F32)
    right[rank:2 * rank, cols:cols + 128] = jnp.where(row == 0, 1.0, 0.0).astype(F32)
    ga_acc[...] = jnp.zeros_like(ga_acc)
    gb_acc[...] = jnp.zeros_like(gb_acc)

    def build(i):
        w_loads[i].wait()
        base = order[i] * cols

        def step(j, carry):
            at = pl.ds(pl.multiple_of(base + j * 128, 128), 128)
            both = contract_first(left[:, at].astype(BF16), right[...].astype(BF16))
            scale = both[:, cols:cols + 128]
            for k in range(cols // 128):
                lanes = slice(k * 128, (k + 1) * 128)
                w[at, lanes] = ((w[at, lanes].astype(F32) + both[:, lanes]) * scale).astype(BF16)
            return carry

        lax.fori_loop(0, cols // 128, step, 0)

    gathered = {}

    def ag0(u):
        mine = x.at[u, own]
        gathered[u] = [
            send(mine, mine, ag_s.at[u, 0], ag_r.at[u, 0], sec, across),
            send(mine, mine, ag_s.at[u, 1], ag_r.at[u, 1], sec, pp),
            send(mine, mine, ag_s.at[u, 2], ag_r.at[u, 2], sec, mm),
        ]

    def ag1(u):
        gathered[u][0].wait_recv()
        part = x.at[u, across]
        gathered[u] += [
            send(part, part, ag_s.at[u, 3], ag_r.at[u, 3], sec, pp),
            send(part, part, ag_s.at[u, 4], ag_r.at[u, 4], sec, mm),
        ]

    def ag2(u):
        gathered[u][1].wait_recv()
        part = x.at[u, mm]
        gathered[u].append(send(part, part, ag_s.at[u, 5], ag_r.at[u, 5], sec, pp))

    def ag3(u):
        gathered[u][4].wait_recv()
        part = x.at[u, po]
        gathered[u].append(send(part, part, ag_s.at[u, 6], ag_r.at[u, 6], sec, mm))

    def fwd(u, which, first=False):
        rows = x[u, which]
        floats = rows.astype(F32)
        squares = floats * floats
        total = squares[:, 0:128]
        for k in range(1, cols // 128):
            total = total + squares[:, k * 128:(k + 1) * 128]
        product = jnp.dot(rows, w[block(which), :], preferred_element_type=F32)
        if first:
            sq[u] = total
            acc[u] = product
        else:
            sq[u] += total
            acc[u] += product

    def fwd_near(u):
        fwd(u, own, True)
        fwd(u, across)
        fwd(u, mm)
        gathered[u][2].wait_recv()
        fwd(u, pp)
        gathered[u][3].wait_recv()
        fwd(u, mo)
        fwd(u, po)

    def fwd_far(u):
        gathered[u][5].wait_recv()
        fwd(u, tt)
        gathered[u][6].wait_recv()
        fwd(u, to)
        inv = lax.rsqrt(jnp.sum(sq[u], axis=1, keepdims=True) / width + EPS)
        yb[u] = (x[u, own].astype(F32) + inv * acc[u]).astype(BF16)
        finish(u, yb.at[u], acts_out, 0)

    shifted, outs, returned = {}, [], []

    def finish(u, result, out, which):
        if u < 2:
            if which == 0:
                shifted[u, 0] = send(result, x.at[u + 2, own], sh_s.at[u, 0], sh_r.at[u, 0], ahead, tp)
            else:
                shifted[u, 1] = send(result, c.at[u + 2], sh_s.at[u, 1], sh_r.at[u, 1], behind, tp)
        tick, relay = u // 2, u % 2
        if relay == 0:
            copy = pltpu.make_async_copy(result, out.at[0, tick, 0], out_sem.at[tick * 2 + which])
            copy.start()
            outs.append(copy)
        else:
            k = tick * 2 + which
            returned.append(send(result, out.at[1, tick, 0], ro_s.at[k], ro_r.at[k], mirror, tp))

    def take_x(u):
        shifted[u, 0].wait_recv()

        @pl.when(sec == 0)
        def _():
            x[u + 2, own] = fa[u]

    def take_c(u):
        shifted[u, 1].wait_recv()

        @pl.when(sec == n_sec - 1)
        def _():
            c[u + 2] = fc[u]

    reduced = {}

    def part(u, which):
        return contract_last(c[u], w[block(which), :])

    def rs_send(u, i, value, to_tp):
        ps[u, i] = value.astype(BF16)
        reduced.setdefault(u, {})[i] = send(
            ps.at[u, i], pr.at[u, i], rs_s.at[u, i], rs_r.at[u, i], sec, to_tp
        )

    def got(u, i):
        reduced[u][i].wait_recv()
        return pr[u, i].astype(F32)

    def rs0(u):
        rs_send(u, 0, part(u, tt), pp)
        rs_send(u, 1, part(u, to), mm)

    def rs1(u):
        rs_send(u, 2, part(u, po), pp)
        rs_send(u, 3, part(u, mm), mm)

    def rs2(u):
        rs_send(u, 4, part(u, pp) + got(u, 0), pp)
        rs_send(u, 5, part(u, mo) + got(u, 1), mm)

    def rs3(u):
        rs_send(u, 6, part(u, across) + got(u, 5) + got(u, 2), across)

    summed = {}

    def split_sum(value):
        ones = jnp.ones((16, cols), BF16)
        high = value.astype(BF16)
        low = (value - high.astype(F32)).astype(BF16)
        return (contract_last(ones, high) + contract_last(ones, low))[0:8]

    def rs4(u):
        total = part(u, own) + got(u, 4) + got(u, 3) + got(u, 6)
        acc_g[u] = total
        floats = s[u].astype(F32)
        at = block(own)
        pair = jnp.concatenate([left[0:rank, at] * left[rank:2 * rank, at], right[0:rank, 0:cols]], axis=0).astype(BF16)
        sm[u, own, 0:8] = contract_last(pair, c[u])[8:16]
        sm[u, own, 8:16] = contract_last(pair, s[u])[0:8]
        sm[u, own, 16:24] = split_sum(floats * floats)
        sm[u, own, 24:32] = split_sum(floats * total)
        mine = sm.at[u, own]
        summed[u] = [
            send(mine, mine, sm_s.at[u, k - 1], sm_r.at[u, k - 1], sec, (tp + k) % n_tp)
            for k in range(1, n_tp)
        ]

    def rs5(u):
        for copy in summed[u]:
            copy.wait_recv()
        total = jnp.sum(sm[u], axis=0)
        low, latent = total[0:8], total[8:16]
        inv = lax.rsqrt(total[16:24] / width + EPS)
        factor = inv * inv * inv * total[24:32] / width
        row8 = lax.broadcasted_iota(jnp.int32, (8, 128), 0)
        turned = jnp.transpose(jnp.where(row8 < 4, inv, factor))
        inv_col, factor_col = turned[:, 0:1], turned[:, 4:5]
        floats = s[u].astype(F32)
        gb[u] = (c[u].astype(F32) + inv_col * acc_g[u] - factor_col * floats).astype(BF16)
        finish(u, gb.at[u], grads_out, 1)
        zeros = jnp.zeros_like(low)
        low16 = jnp.concatenate([low * inv, zeros], axis=0).astype(BF16)
        latent16 = jnp.concatenate([latent * inv, zeros], axis=0).astype(BF16)
        ga_acc[...] += jnp.dot(low16, s[u], preferred_element_type=F32)[0:8]
        gb_acc[...] += jnp.dot(latent16, c[u], preferred_element_type=F32)[0:8]

    loads[0].wait()
    ag0(D0)
    loads[1].wait()
    build(0)
    build(1)
    rs0(D0)
    build(2)
    build(3)
    rs1(D0)
    ag1(D0)
    build(4)
    build(5)
    ag2(D0)
    rs2(D0)
    ag3(D0)
    build(6)
    rs3(D0)
    build(7)
    rev_c.wait_recv()
    rs0(U0)
    rs1(U0)
    rev_x.wait_recv()
    ag0(U0)
    for copy in loads[2:]:
        copy.wait()
    fwd_near(D0)
    rs4(D0)
    fwd_far(D0)
    ag1(U0)
    rs2(U0)
    ag2(U0)
    rs5(D0)
    rs3(U0)
    ag3(U0)
    rev_s[U0].wait_recv()
    rs4(U0)
    fwd_near(U0)
    rs5(U0)
    take_c(D0)
    rs0(D1)
    fwd_far(U0)
    rs1(D1)
    take_c(U0)
    rs0(U1)
    rs1(U1)
    take_x(U0)
    ag0(U1)
    rs2(D1)
    rs2(U1)
    ag1(U1)
    rs3(U1)
    ag2(U1)
    rs3(D1)
    ag3(U1)
    rev_s[U1].wait_recv()
    rs4(U1)
    take_x(D0)
    ag0(D1)
    fwd_near(U1)
    rs5(U1)
    fwd_far(U1)
    ag1(D1)
    ag2(D1)
    ag3(D1)
    rs4(D1)
    fwd_near(D1)
    rs5(D1)
    gar[own] = ga_acc[...] * left[rank:2 * rank, block(own)]
    mine = gar.at[own]
    shares = [
        send(mine, mine, ga_s.at[k - 1], ga_r.at[k - 1], sec, (tp + k) % n_tp)
        for k in range(1, n_tp)
    ]
    grad_b[0] = gb_acc[...].astype(BF16)
    fwd_far(D1)
    for copy in shares:
        copy.wait_recv()
    for k in range(n_tp):
        grad_a[0, :, k * cols:(k + 1) * cols] = gar[k].astype(BF16)
    for copy in outs:
        copy.wait()
    for copy in returned:
        copy.wait_recv()
    for copy in sends:
        copy.wait_send()


def body(acts_in, cots_in, stash, fresh_acts, fresh_cots, gains, weights, adapter_a, adapter_b):
    rows, cols = acts_in.shape[2], acts_in.shape[3]
    ticks = stash.shape[1]
    rank, width = adapter_a.shape[1], adapter_a.shape[2]
    n_tp = width // cols
    units = 2 * ticks
    hbm, vmem = pl.BlockSpec(memory_space=pl.ANY), pl.BlockSpec(memory_space=pltpu.VMEM)
    dma = pltpu.SemaphoreType.DMA
    tile = (rows, cols)
    out = jax.ShapeDtypeStruct((2, ticks, 1, rows, cols), BF16)
    return pl.pallas_call(
        kernel,
        name="relays",
        out_shape=(
            out,
            out,
            jax.ShapeDtypeStruct((1, rank, width), BF16),
            jax.ShapeDtypeStruct((1, rank, cols), BF16),
        ),
        in_specs=[hbm, hbm, hbm, hbm, hbm, vmem, hbm, vmem, vmem],
        out_specs=(hbm, hbm, vmem, vmem),
        scratch_shapes=[
            pltpu.VMEM((width, cols), BF16),
            pltpu.VMEM((units, n_tp) + tile, BF16),
            pltpu.VMEM((units,) + tile, BF16),
            pltpu.VMEM((units,) + tile, BF16),
            pltpu.VMEM((2,) + tile, BF16),
            pltpu.VMEM((2,) + tile, BF16),
            pltpu.VMEM((units, 7) + tile, BF16),
            pltpu.VMEM((units, 7) + tile, BF16),
            pltpu.VMEM((units,) + tile, BF16),
            pltpu.VMEM((units,) + tile, BF16),
            pltpu.VMEM((units, n_tp, 32, rows), F32),
            pltpu.VMEM((n_tp, rank, cols), F32),
            pltpu.VMEM((units,) + tile, F32),
            pltpu.VMEM((units,) + tile, F32),
            pltpu.VMEM((units, rows, 128), F32),
            pltpu.VMEM((2 * rank, width), F32),
            pltpu.VMEM((2 * rank, cols + 128), F32),
            pltpu.VMEM((rank, cols), F32),
            pltpu.VMEM((rank, cols), F32),
            dma((n_tp,)),
            dma((6,)),
            dma((4,)),
            dma((units, 7)),
            dma((units, 7)),
            dma((units, 7)),
            dma((units, 7)),
            dma((units, 7)),
            dma((units, 7)),
            dma((2, 2)),
            dma((2, 2)),
            dma((4,)),
            dma((4,)),
            dma((4,)),
            dma((4,)),
            dma((7,)),
            dma((7,)),
        ],
        compiler_params=pltpu.CompilerParams(
            collective_id=0, has_side_effects=True, vmem_limit_bytes=56 * 1024 * 1024
        ),
    )(acts_in, cots_in, stash, fresh_acts, fresh_cots, gains, weights, adapter_a, adapter_b)


def solution(mesh):
    in_specs = (
        P(None, "section", None, "tp"),
        P(None, "section", None, "tp"),
        P(None, None, "section", None, "tp"),
        P(None, None, None, "tp"),
        P(None, None, None, "tp"),
        P("section", None),
        P("section", None, "tp"),
        P("section", None, None),
        P("section", None, "tp"),
    )
    out_specs = (
        P(None, None, "section", None, "tp"),
        P(None, None, "section", None, "tp"),
        P("section", None, None),
        P("section", None, "tp"),
    )
    return jax.shard_map(body, mesh=mesh, in_specs=in_specs, out_specs=out_specs, check_vma=False)
```

```python
import jax
import jax.numpy as jnp
from jax import lax
from jax.experimental import pallas as pl
from jax.experimental.pallas import tpu as pltpu
from jax.sharding import PartitionSpec as P

EPS = 1e-05
MESH = pl.DeviceIdType.MESH
F32 = jnp.float32
BF16 = jnp.bfloat16

D0, U0, D1, U1 = range(4)

SCHEDULE = (
    ("rev_x", 1), ("ag0", 0), ("build", 0), ("build", 2), ("build", 1), ("r0a", 0), ("r0b", 0), ("ag2b", 0),
    ("ag2a", 0), ("build", 7), ("rev_c", 1), ("ag1", 0), ("ag0", 1), ("ag1", 1), ("build", 3), ("ag3", 0),
    ("r1a", 0), ("ag2a", 1), ("build", 6), ("ag2b", 1), ("send_s", 1), ("r0a", 1), ("r0b", 1), ("build", 5),
    ("build", 4), ("r2b", 0), ("ag3", 1), ("f0", 1), ("f2", 1), ("r1a", 1), ("f1", 1), ("r2b", 1),
    ("r3", 0), ("f0", 0), ("f1", 0), ("r2a", 0), ("r2a", 1), ("r1b", 0), ("f3", 1), ("ox", 1),
    ("f2", 0), ("r3", 1), ("r1b", 1), ("f3", 0), ("ag0", 3), ("r4", 0), ("r4", 1), ("ag0", 2),
    ("r5", 0), ("ag1", 3), ("r5", 1), ("oc", 1), ("r0a", 2), ("ag2b", 3), ("ag2a", 3), ("r0a", 3),
    ("r0b", 3), ("ag3", 3), ("r0b", 2), ("r1a", 3), ("send_s", 3), ("r2b", 3), ("f0", 3), ("r2a", 3),
    ("f0", 2), ("r1b", 3), ("r3", 3), ("r2b", 2), ("f2", 3), ("f1", 3), ("r1a", 2), ("f3", 3),
    ("ox", 3), ("r4", 3), ("r2a", 2), ("r1b", 2), ("r3", 2), ("r5", 3), ("oc", 3), ("ag2a", 2),
    ("ag2b", 2), ("r4", 2), ("ag1", 2), ("ag3", 2), ("r5", 2), ("f1", 2), ("f2", 2), ("f3", 2),
)


def contract_last(left, right):
    return lax.dot_general(left, right, (((1,), (1,)), ((), ())), preferred_element_type=F32)


def contract_first(left, right):
    return lax.dot_general(left, right, (((0,), (0,)), ((), ())), preferred_element_type=F32)


def kernel(
    acts, cots, stash, fresh_acts, fresh_cots, gain, weights, lower, upper,
    acts_out, grads_out, grad_a, grad_b,
    w, x, c, s, fa, fc, ps, pr, yb, gb, sm, gar, acc, acc_g, sq, left, right, ga_acc, gb_acc,
    w_sem, in_sem, out_sem,
    ag_s, ag_r, rs_s, rs_r, sm_s, sm_r, sh_s, sh_r, ri_s, ri_r, ro_s, ro_r, ga_s, ga_r,
):
    sec, tp = lax.axis_index("section"), lax.axis_index("tp")
    n_sec, n_tp = lax.axis_size("section"), lax.axis_size("tp")
    cols = w.shape[1]
    width = n_tp * cols
    rank = lower.shape[1]
    nx = n_tp // 2
    xi, yi = tp // 2, tp % 2
    turn = 1 - 2 * yi
    xp, xm, x2 = (xi + turn + nx) % nx, (xi - turn + nx) % nx, (xi + 2) % nx
    yo = 1 - yi
    own, across = tp, xi * 2 + yo
    pp, po, mm, mo, tt, to = xp * 2 + yi, xp * 2 + yo, xm * 2 + yi, xm * 2 + yo, x2 * 2 + yi, x2 * 2 + yo
    ahead, behind, mirror = (sec + 1) % n_sec, (sec + n_sec - 1) % n_sec, n_sec - 1 - sec
    sends = []

    def send(src, dst, send_sem, recv_sem, to_sec, to_tp):
        copy = pltpu.make_async_remote_copy(
            src_ref=src, dst_ref=dst, send_sem=send_sem, recv_sem=recv_sem,
            device_id=(to_sec, to_tp), device_id_type=MESH,
        )
        copy.start()
        sends.append(copy)
        return copy

    def block(index):
        return pl.ds(pl.multiple_of(index * cols, cols), cols)

    order = (tt, to, po, mm, pp, mo, across, own)
    loads = [
        pltpu.make_async_copy(acts.at[0, 0], x.at[D0, own], in_sem.at[0]),
        pltpu.make_async_copy(cots.at[0, 0], c.at[D0], in_sem.at[1]),
    ]
    w_loads = [
        pltpu.make_async_copy(weights.at[0, block(which)], w.at[block(which)], w_sem.at[i])
        for i, which in enumerate(order)
    ]
    loads += [
        pltpu.make_async_copy(stash.at[0, 0, 0], s.at[D0], in_sem.at[2]),
        pltpu.make_async_copy(stash.at[0, 1, 0], s.at[D1], in_sem.at[3]),
        pltpu.make_async_copy(fresh_acts.at[:, 0], fa, in_sem.at[4]),
        pltpu.make_async_copy(fresh_cots.at[:, 0], fc, in_sem.at[5]),
    ]
    for copy in loads[:2] + w_loads + loads[2:]:
        copy.start()

    barrier = pltpu.get_barrier_semaphore()
    peers = [(sec, (tp + k) % n_tp) for k in range(1, n_tp)]
    peers += [(mirror, tp), (ahead, tp), (behind, tp)]
    for peer in peers:
        pl.semaphore_signal(barrier, inc=1, device_id=peer, device_id_type=MESH)
    pl.semaphore_wait(barrier, len(peers))

    turned_in = {}

    def rev_c(u):
        turned_in["c"] = send(cots.at[1, 0], c.at[u], ri_s.at[0], ri_r.at[0], mirror, tp)

    def rev_x(u):
        turned_in["x"] = send(acts.at[1, 0], x.at[u, own], ri_s.at[1], ri_r.at[1], mirror, tp)

    def rev_s(u):
        tick = u // 2
        turned_in[u] = send(stash.at[1, tick, 0], s.at[u], ri_s.at[2 + tick], ri_r.at[2 + tick], mirror, tp)

    left[0:rank] = lower[0].astype(F32)
    left[rank:2 * rank] = jnp.broadcast_to(gain[...].astype(F32), (rank, width))
    row = lax.broadcasted_iota(jnp.int32, (rank, 128), 0)
    right[0:rank, 0:cols] = upper[0].astype(F32)
    right[rank:2 * rank, 0:cols] = jnp.zeros((rank, cols), F32)
    right[0:rank, cols:cols + 128] = jnp.zeros((rank, 128), F32)
    right[rank:2 * rank, cols:cols + 128] = jnp.where(row == 0, 1.0, 0.0).astype(F32)
    ga_acc[...] = jnp.zeros_like(ga_acc)
    gb_acc[...] = jnp.zeros_like(gb_acc)

    def build(i):
        w_loads[i].wait()
        base = order[i] * cols

        def step(j, carry):
            at = pl.ds(pl.multiple_of(base + j * 128, 128), 128)
            both = contract_first(left[:, at].astype(BF16), right[...].astype(BF16))
            scale = both[:, cols:cols + 128]
            for k in range(cols // 128):
                lanes = slice(k * 128, (k + 1) * 128)
                w[at, lanes] = ((w[at, lanes].astype(F32) + both[:, lanes]) * scale).astype(BF16)
            return carry

        lax.fori_loop(0, cols // 128, step, 0)

    gathered, here = {}, set()

    def arrive(u, i):
        if (u, i) not in here:
            here.add((u, i))
            gathered[u][i].wait_recv()

    def ag0(u):
        mine = x.at[u, own]
        gathered[u] = {
            i: send(mine, mine, ag_s.at[u, i], ag_r.at[u, i], sec, to_tp)
            for i, to_tp in enumerate((across, pp, mm))
        }

    def ag1(u):
        arrive(u, 0)
        part = x.at[u, across]
        for i, to_tp in ((3, pp), (4, mm)):
            gathered[u][i] = send(part, part, ag_s.at[u, i], ag_r.at[u, i], sec, to_tp)

    def ag2(u, k, wait, which, to_tp):
        half = x.shape[2] // 2
        arrive(u, wait)
        piece = x.at[u, which, pl.ds(k * half, half)]
        gathered[u][5 + k] = send(piece, piece, ag_s.at[u, 5 + k], ag_r.at[u, 5 + k], sec, to_tp)

    def ag2a(u):
        ag2(u, 0, 1, mm, pp)

    def ag2b(u):
        ag2(u, 1, 2, pp, mm)

    def ag3(u):
        arrive(u, 5)
        arrive(u, 6)
        far = x.at[u, tt]
        gathered[u][7] = send(far, far, ag_s.at[u, 7], ag_r.at[u, 7], sec, across)

    def fwd(u, which, first=False):
        rows = x[u, which]
        floats = rows.astype(F32)
        squares = floats * floats
        total = squares[:, 0:128]
        for k in range(1, cols // 128):
            total = total + squares[:, k * 128:(k + 1) * 128]
        product = jnp.dot(rows, w[block(which), :], preferred_element_type=F32)
        if first:
            sq[u] = total
            acc[u] = product
        else:
            sq[u] += total
            acc[u] += product

    def f0(u):
        fwd(u, own, True)
        for i, which in ((1, mm), (2, pp), (0, across)):
            arrive(u, i)
            fwd(u, which)

    def f1(u):
        for i, which in ((3, mo), (4, po)):
            arrive(u, i)
            fwd(u, which)

    def f2(u):
        arrive(u, 5)
        arrive(u, 6)
        fwd(u, tt)

    def f3(u):
        arrive(u, 7)
        fwd(u, to)
        inv = lax.rsqrt(jnp.sum(sq[u], axis=1, keepdims=True) / width + EPS)
        yb[u] = (x[u, own].astype(F32) + inv * acc[u]).astype(BF16)
        finish(u, yb.at[u], acts_out, 0)

    shifted, outs, returned = {}, [], []

    def finish(u, result, out, which):
        if u < 2:
            if which == 0:
                shifted[u, 0] = send(result, x.at[u + 2, own], sh_s.at[u, 0], sh_r.at[u, 0], ahead, tp)
            else:
                shifted[u, 1] = send(result, c.at[u + 2], sh_s.at[u, 1], sh_r.at[u, 1], behind, tp)
        tick, relay = u // 2, u % 2
        if relay == 0:
            copy = pltpu.make_async_copy(result, out.at[0, tick, 0], out_sem.at[tick * 2 + which])
            copy.start()
            outs.append(copy)

    def turn_out(u, result, out, which):
        tick = u // 2
        k = tick * 2 + which
        returned.append(send(result, out.at[1, tick, 0], ro_s.at[k], ro_r.at[k], mirror, tp))

    def ox(u):
        turn_out(u, yb.at[u], acts_out, 0)

    def oc(u):
        turn_out(u, gb.at[u], grads_out, 1)

    taken = set()

    def fresh(i):
        if i not in taken:
            taken.add(i)
            loads[i].wait()

    def take_x(u):
        shifted[u, 0].wait_recv()
        fresh(4)

        @pl.when(sec == 0)
        def _():
            x[u + 2, own] = fa[u]

    def take_c(u):
        shifted[u, 1].wait_recv()
        fresh(5)

        @pl.when(sec == n_sec - 1)
        def _():
            c[u + 2] = fc[u]

    reduced = {}

    def part(u, which):
        return contract_last(c[u], w[block(which), :])

    def rs_send(u, i, value, to_tp):
        ps[u, i] = value.astype(BF16)
        reduced.setdefault(u, {})[i] = send(
            ps.at[u, i], pr.at[u, i], rs_s.at[u, i], rs_r.at[u, i], sec, to_tp
        )

    def got(u, i):
        reduced[u][i].wait_recv()
        return pr[u, i].astype(F32)

    def r0a(u):
        rs_send(u, 0, part(u, tt), pp)

    def r0b(u):
        rs_send(u, 1, part(u, to), mm)

    def r1a(u):
        rs_send(u, 2, part(u, po), pp)

    def r1b(u):
        rs_send(u, 3, part(u, mm), mm)

    def r2a(u):
        rs_send(u, 4, part(u, pp) + got(u, 0), pp)

    def r2b(u):
        rs_send(u, 5, part(u, mo) + got(u, 1), mm)

    def r3(u):
        rs_send(u, 6, part(u, across) + got(u, 5) + got(u, 2), across)

    summed = {}
    row8 = lax.broadcasted_iota(jnp.int32, (8, 128), 0)

    def three_terms(value):
        first = value.astype(BF16).astype(F32)
        second = (value - first).astype(BF16).astype(F32)
        third = value - first - second
        return jnp.where(row8 == 0, first, jnp.where(row8 == 1, second, jnp.where(row8 == 2, third, 0.0)))

    def split_sum(value):
        ones = jnp.ones((16, cols), BF16)
        high = value.astype(BF16)
        low = (value - high.astype(F32)).astype(BF16)
        return (contract_last(ones, high) + contract_last(ones, low))[0:8]

    def r4(u):
        floats = s[u].astype(F32)
        at = block(own)
        pair = jnp.concatenate([left[0:rank, at] * left[rank:2 * rank, at], right[0:rank, 0:cols]], axis=0).astype(BF16)
        sm[u, own, 0:16] = jnp.concatenate(
            [contract_last(pair, c[u])[8:16], contract_last(pair, s[u])[0:8]], axis=0
        ).astype(BF16)
        squares = three_terms(split_sum(floats * floats))
        total = part(u, own) + got(u, 4) + got(u, 3) + got(u, 6)
        acc_g[u] = total
        crossed = three_terms(split_sum(s[u].astype(F32) * total))
        sm[u, own, 16:32] = jnp.concatenate([squares, crossed], axis=0).astype(BF16)
        mine = sm.at[u, own]
        summed[u] = [
            send(mine, mine, sm_s.at[u, k - 1], sm_r.at[u, k - 1], sec, (tp + k) % n_tp)
            for k in range(1, n_tp)
        ]

    def r5(u):
        for copy in summed[u]:
            copy.wait_recv()
        total = jnp.sum(sm[u].astype(F32), axis=0)
        low, latent = total[0:8], total[8:16]
        inv = lax.rsqrt(jnp.sum(total[16:24], axis=0, keepdims=True) / width + EPS)
        factor = inv * inv * inv * jnp.sum(total[24:32], axis=0, keepdims=True) / width
        turned = jnp.transpose(jnp.where(row8 < 4, inv, factor))
        inv_col, factor_col = turned[:, 0:1], turned[:, 4:5]
        floats = s[u].astype(F32)
        gb[u] = (c[u].astype(F32) + inv_col * acc_g[u] - factor_col * floats).astype(BF16)
        finish(u, gb.at[u], grads_out, 1)
        zeros = jnp.zeros_like(low)
        low16 = jnp.concatenate([low * inv, zeros], axis=0).astype(BF16)
        latent16 = jnp.concatenate([latent * inv, zeros], axis=0).astype(BF16)
        ga_acc[...] += jnp.dot(low16, s[u], preferred_element_type=F32)[0:8]
        gb_acc[...] += jnp.dot(latent16, c[u], preferred_element_type=F32)[0:8]

    def begin_c(u):
        if u == D0:
            loads[1].wait()
        elif u == U0:
            turned_in["c"].wait_recv()
        else:
            take_c(u - 2)
        r0a(u)

    def begin_x(u):
        if u == D0:
            loads[0].wait()
        elif u == U0:
            turned_in["x"].wait_recv()
        else:
            take_x(u - 2)
        ag0(u)

    def begin_s(u):
        if u in (U0, U1):
            turned_in[u].wait_recv()
        else:
            loads[2 + u // 2].wait()
        r4(u)

    shares = []

    def share_a():
        gar[own] = ga_acc[...] * left[rank:2 * rank, block(own)]
        mine = gar.at[own]
        for k in range(1, n_tp):
            shares.append(send(mine, mine, ga_s.at[k - 1], ga_r.at[k - 1], sec, (tp + k) % n_tp))
        grad_b[0] = gb_acc[...]

    steps = {
        "build": build, "rev_c": rev_c, "rev_x": rev_x, "send_s": rev_s,
        "ag0": begin_x, "ag1": ag1, "ag2a": ag2a, "ag2b": ag2b, "ag3": ag3,
        "f0": f0, "f1": f1, "f2": f2, "f3": f3,
        "r0a": begin_c, "r0b": r0b, "r1a": r1a, "r1b": r1b, "r2a": r2a, "r2b": r2b, "r3": r3,
        "r4": begin_s, "r5": r5, "ox": ox, "oc": oc,
    }
    last = [which for which in SCHEDULE if which[0] == "r5"][-1]
    for step, u in SCHEDULE:
        steps[step](u)
        if (step, u) == last:
            share_a()
    for copy in shares:
        copy.wait_recv()
    for k in range(n_tp):
        grad_a[0, :, k * cols:(k + 1) * cols] = gar[k]
    for copy in outs:
        copy.wait()
    for copy in returned:
        copy.wait_recv()
    for copy in sends:
        copy.wait_send()


def settle(acts, grads, sum_a, sum_b, acts_out, grads_out, grad_a, grad_b, held, sem_in, sem_out):
    pairs = [(src, dst, r, k) for r in range(2) for k in range(acts.shape[1]) for src, dst in ((acts, acts_out), (grads, grads_out))]
    takes = [pltpu.make_async_copy(src.at[r, k, 0], held.at[i], sem_in.at[i]) for i, (src, dst, r, k) in enumerate(pairs)]
    gives = [pltpu.make_async_copy(held.at[i], dst.at[r, k, 0], sem_out.at[i]) for i, (src, dst, r, k) in enumerate(pairs)]
    for take in takes:
        take.start()
    grad_a[...] = sum_a[...].astype(BF16)
    grad_b[...] = sum_b[...].astype(BF16)
    for take, give in zip(takes, gives):
        take.wait()
        give.start()
    for give in gives:
        give.wait()


def body(acts_in, cots_in, stash, fresh_acts, fresh_cots, gains, weights, adapter_a, adapter_b):
    rows, cols = acts_in.shape[2], acts_in.shape[3]
    ticks = stash.shape[1]
    rank, width = adapter_a.shape[1], adapter_a.shape[2]
    n_tp = width // cols
    units = 2 * ticks
    hbm, vmem = pl.BlockSpec(memory_space=pl.ANY), pl.BlockSpec(memory_space=pltpu.VMEM)
    dma = pltpu.SemaphoreType.DMA
    tile = (rows, cols)
    out = jax.ShapeDtypeStruct((2, ticks, 1, rows, cols), BF16)
    results = pl.pallas_call(
        kernel,
        name="relays",
        out_shape=(
            out,
            out,
            jax.ShapeDtypeStruct((1, rank, width), F32),
            jax.ShapeDtypeStruct((1, rank, cols), F32),
        ),
        in_specs=[hbm, hbm, hbm, hbm, hbm, vmem, hbm, vmem, vmem],
        out_specs=(hbm, hbm, vmem, vmem),
        scratch_shapes=[
            pltpu.VMEM((width, cols), BF16),
            pltpu.VMEM((units, n_tp) + tile, BF16),
            pltpu.VMEM((units,) + tile, BF16),
            pltpu.VMEM((units,) + tile, BF16),
            pltpu.VMEM((2,) + tile, BF16),
            pltpu.VMEM((2,) + tile, BF16),
            pltpu.VMEM((units, 7) + tile, BF16),
            pltpu.VMEM((units, 7) + tile, BF16),
            pltpu.VMEM((units,) + tile, BF16),
            pltpu.VMEM((units,) + tile, BF16),
            pltpu.VMEM((units, n_tp, 32, rows), BF16),
            pltpu.VMEM((n_tp, rank, cols), F32),
            pltpu.VMEM((units,) + tile, F32),
            pltpu.VMEM((units,) + tile, F32),
            pltpu.VMEM((units, rows, 128), F32),
            pltpu.VMEM((2 * rank, width), F32),
            pltpu.VMEM((2 * rank, cols + 128), F32),
            pltpu.VMEM((rank, cols), F32),
            pltpu.VMEM((rank, cols), F32),
            dma((n_tp,)),
            dma((6,)),
            dma((4,)),
            dma((units, 8)),
            dma((units, 8)),
            dma((units, 7)),
            dma((units, 7)),
            dma((units, 7)),
            dma((units, 7)),
            dma((2, 2)),
            dma((2, 2)),
            dma((4,)),
            dma((4,)),
            dma((4,)),
            dma((4,)),
            dma((7,)),
            dma((7,)),
        ],
        compiler_params=pltpu.CompilerParams(
            collective_id=0, has_side_effects=True, vmem_limit_bytes=56 * 1024 * 1024
        ),
    )(acts_in, cots_in, stash, fresh_acts, fresh_cots, gains, weights, adapter_a, adapter_b)
    return pl.pallas_call(
        settle,
        name="settle",
        out_shape=(
            out,
            out,
            jax.ShapeDtypeStruct((1, rank, width), BF16),
            jax.ShapeDtypeStruct((1, rank, cols), BF16),
        ),
        in_specs=[hbm, hbm, vmem, vmem],
        out_specs=(hbm, hbm, vmem, vmem),
        scratch_shapes=[pltpu.VMEM((4 * ticks,) + tile, BF16), dma((4 * ticks,)), dma((4 * ticks,))],
    )(*results)


def solution(mesh):
    in_specs = (
        P(None, "section", None, "tp"),
        P(None, "section", None, "tp"),
        P(None, None, "section", None, "tp"),
        P(None, None, None, "tp"),
        P(None, None, None, "tp"),
        P("section", None),
        P("section", None, "tp"),
        P("section", None, None),
        P("section", None, "tp"),
    )
    out_specs = (
        P(None, None, "section", None, "tp"),
        P(None, None, "section", None, "tp"),
        P("section", None, None),
        P("section", None, "tp"),
    )
    return jax.shard_map(body, mesh=mesh, in_specs=in_specs, out_specs=out_specs, check_vma=False)
```

```python
import jax
import jax.numpy as jnp
from jax import lax
from jax.experimental import pallas as pl
from jax.experimental.pallas import tpu as pltpu
from jax.sharding import PartitionSpec as P

EPS = 1e-05
MESH = pl.DeviceIdType.MESH
F32 = jnp.float32
BF16 = jnp.bfloat16

D0, U0, D1, U1 = range(4)

SCHEDULE = (
    ("ag0", 0), ("rev_x", 1), ("build", 0), ("r0a", 0), ("build", 1), ("ag2b", 0), ("r0b", 0), ("build", 3),
    ("ag2a", 0), ("build", 2), ("ag0", 1), ("rev_c", 1), ("build", 5), ("r1a", 0), ("build", 4), ("r2b", 0),
    ("build", 7), ("r1b", 0), ("r2a", 0), ("build", 6), ("r0a", 1), ("r3", 0), ("r0b", 1), ("f0", 0),
    ("r4", 0), ("ag2b", 1), ("send_s", 1), ("ag3", 0), ("ag2a", 1), ("r1a", 1), ("r2b", 1), ("ag1", 1),
    ("f2", 0), ("f0", 1), ("r5", 0), ("ag3", 1), ("f2", 1), ("r2a", 1), ("r1b", 1), ("r3", 1),
    ("ag1", 0), ("r0a", 2), ("f1", 1), ("r0b", 2), ("r4", 1), ("f3", 1), ("r1b", 2), ("send_s", 3),
    ("r1a", 2), ("r5", 1), ("ag0", 3), ("ox", 1), ("r2b", 2), ("r0a", 3), ("ag2a", 3), ("oc", 1),
    ("r0b", 3), ("f1", 0), ("r1a", 3), ("f0", 3), ("ag2b", 3), ("r3", 2), ("r2b", 3), ("ag3", 3),
    ("ag1", 3), ("f3", 0), ("f2", 3), ("r2a", 3), ("r3", 3), ("r1b", 3), ("r2a", 2), ("f1", 3),
    ("f3", 3), ("ox", 3), ("r4", 3), ("ag0", 2), ("r4", 2), ("r5", 3), ("oc", 3), ("ag2b", 2),
    ("ag2a", 2), ("r5", 2), ("ag1", 2), ("ag3", 2), ("f0", 2), ("f2", 2), ("f1", 2), ("f3", 2),
)


def contract_last(left, right):
    return lax.dot_general(left, right, (((1,), (1,)), ((), ())), preferred_element_type=F32)


def contract_first(left, right):
    return lax.dot_general(left, right, (((0,), (0,)), ((), ())), preferred_element_type=F32)


def kernel(
    acts, cots, stash, fresh_acts, fresh_cots, gain, weights, lower, upper,
    acts_out, grads_out, grad_a, grad_b,
    w, x, c, s, fa, fc, ps, pr, yb, gb, sm, gar, acc, acc_g, sq, left, right, ga_acc, gb_acc,
    w_sem, in_sem, out_sem,
    ag_s, ag_r, rs_s, rs_r, sm_s, sm_r, sh_s, sh_r, ri_s, ri_r, ro_s, ro_r, ga_s, ga_r,
):
    sec, tp = lax.axis_index("section"), lax.axis_index("tp")
    n_sec, n_tp = lax.axis_size("section"), lax.axis_size("tp")
    cols = w.shape[1]
    width = n_tp * cols
    rank = lower.shape[1]
    nx = n_tp // 2
    xi, yi = tp // 2, tp % 2
    turn = 1 - 2 * yi
    xp, xm, x2 = (xi + turn + nx) % nx, (xi - turn + nx) % nx, (xi + 2) % nx
    yo = 1 - yi
    own, across = tp, xi * 2 + yo
    pp, po, mm, mo, tt, to = xp * 2 + yi, xp * 2 + yo, xm * 2 + yi, xm * 2 + yo, x2 * 2 + yi, x2 * 2 + yo
    ahead, behind, mirror = (sec + 1) % n_sec, (sec + n_sec - 1) % n_sec, n_sec - 1 - sec
    sends = []

    def send(src, dst, send_sem, recv_sem, to_sec, to_tp):
        copy = pltpu.make_async_remote_copy(
            src_ref=src, dst_ref=dst, send_sem=send_sem, recv_sem=recv_sem,
            device_id=(to_sec, to_tp), device_id_type=MESH,
        )
        copy.start()
        sends.append(copy)
        return copy

    def block(index):
        return pl.ds(pl.multiple_of(index * cols, cols), cols)

    order = (tt, to, po, mm, pp, mo, across, own)
    loads = [
        pltpu.make_async_copy(acts.at[0, 0], x.at[D0, own], in_sem.at[0]),
        pltpu.make_async_copy(cots.at[0, 0], c.at[D0], in_sem.at[1]),
    ]
    w_loads = [
        pltpu.make_async_copy(weights.at[0, block(which)], w.at[block(which)], w_sem.at[i])
        for i, which in enumerate(order)
    ]
    loads += [
        pltpu.make_async_copy(stash.at[0, 0, 0], s.at[D0], in_sem.at[2]),
        pltpu.make_async_copy(stash.at[0, 1, 0], s.at[D1], in_sem.at[3]),
        pltpu.make_async_copy(fresh_acts.at[:, 0], fa, in_sem.at[4]),
        pltpu.make_async_copy(fresh_cots.at[:, 0], fc, in_sem.at[5]),
    ]
    for copy in loads[:2] + w_loads + loads[2:]:
        copy.start()

    barrier = pltpu.get_barrier_semaphore()
    peers = [(sec, (tp + k) % n_tp) for k in range(1, n_tp)]
    peers += [(mirror, tp), (ahead, tp), (behind, tp)]
    for peer in peers:
        pl.semaphore_signal(barrier, inc=1, device_id=peer, device_id_type=MESH)
    pl.semaphore_wait(barrier, len(peers))

    turned_in = {}

    def rev_c(u):
        turned_in["c"] = send(cots.at[1, 0], c.at[u], ri_s.at[0], ri_r.at[0], mirror, tp)

    def rev_x(u):
        turned_in["x"] = send(acts.at[1, 0], x.at[u, own], ri_s.at[1], ri_r.at[1], mirror, tp)

    def rev_s(u):
        tick = u // 2
        turned_in[u] = send(stash.at[1, tick, 0], s.at[u], ri_s.at[2 + tick], ri_r.at[2 + tick], mirror, tp)

    left[0:rank] = lower[0].astype(F32)
    left[rank:2 * rank] = jnp.broadcast_to(gain[...].astype(F32), (rank, width))
    row = lax.broadcasted_iota(jnp.int32, (rank, 128), 0)
    right[0:rank, 0:cols] = upper[0].astype(F32)
    right[rank:2 * rank, 0:cols] = jnp.zeros((rank, cols), F32)
    right[0:rank, cols:cols + 128] = jnp.zeros((rank, 128), F32)
    right[rank:2 * rank, cols:cols + 128] = jnp.where(row == 0, 1.0, 0.0).astype(F32)
    ga_acc[...] = jnp.zeros_like(ga_acc)
    gb_acc[...] = jnp.zeros_like(gb_acc)

    def build(i):
        w_loads[i].wait()
        base = order[i] * cols

        def step(j, carry):
            at = pl.ds(pl.multiple_of(base + j * 128, 128), 128)
            both = contract_first(left[:, at].astype(BF16), right[...].astype(BF16))
            scale = both[:, cols:cols + 128]
            for k in range(cols // 128):
                lanes = slice(k * 128, (k + 1) * 128)
                w[at, lanes] = ((w[at, lanes].astype(F32) + both[:, lanes]) * scale).astype(BF16)
            return carry

        lax.fori_loop(0, cols // 128, step, 0)

    gathered, here = {}, set()

    def arrive(u, i):
        if (u, i) not in here:
            here.add((u, i))
            gathered[u][i].wait_recv()

    def ag0(u):
        mine = x.at[u, own]
        gathered[u] = {
            i: send(mine, mine, ag_s.at[u, i], ag_r.at[u, i], sec, to_tp)
            for i, to_tp in enumerate((across, pp, mm))
        }

    def ag1(u):
        arrive(u, 0)
        part = x.at[u, across]
        for i, to_tp in ((3, pp), (4, mm)):
            gathered[u][i] = send(part, part, ag_s.at[u, i], ag_r.at[u, i], sec, to_tp)

    def ag2(u, k, wait, which, to_tp):
        half = x.shape[2] // 2
        arrive(u, wait)
        piece = x.at[u, which, pl.ds(k * half, half)]
        gathered[u][5 + k] = send(piece, piece, ag_s.at[u, 5 + k], ag_r.at[u, 5 + k], sec, to_tp)

    def ag2a(u):
        ag2(u, 0, 1, mm, pp)

    def ag2b(u):
        ag2(u, 1, 2, pp, mm)

    def ag3(u):
        arrive(u, 5)
        arrive(u, 6)
        far = x.at[u, tt]
        gathered[u][7] = send(far, far, ag_s.at[u, 7], ag_r.at[u, 7], sec, across)

    def fwd(u, which, first=False):
        rows = x[u, which]
        floats = rows.astype(F32)
        squares = floats * floats
        total = squares[:, 0:128]
        for k in range(1, cols // 128):
            total = total + squares[:, k * 128:(k + 1) * 128]
        product = jnp.dot(rows, w[block(which), :], preferred_element_type=F32)
        if first:
            sq[u] = total
            acc[u] = product
        else:
            sq[u] += total
            acc[u] += product

    def f0(u):
        fwd(u, own, True)
        for i, which in ((1, mm), (2, pp), (0, across)):
            arrive(u, i)
            fwd(u, which)

    def f1(u):
        for i, which in ((3, mo), (4, po)):
            arrive(u, i)
            fwd(u, which)

    def f2(u):
        arrive(u, 5)
        arrive(u, 6)
        fwd(u, tt)

    def f3(u):
        arrive(u, 7)
        fwd(u, to)
        inv = lax.rsqrt(jnp.sum(sq[u], axis=1, keepdims=True) / width + EPS)
        yb[u] = (x[u, own].astype(F32) + inv * acc[u]).astype(BF16)
        finish(u, yb.at[u], acts_out, 0)

    shifted, outs, returned = {}, [], []

    def finish(u, result, out, which):
        if u < 2:
            if which == 0:
                shifted[u, 0] = send(result, x.at[u + 2, own], sh_s.at[u, 0], sh_r.at[u, 0], ahead, tp)
            else:
                shifted[u, 1] = send(result, c.at[u + 2], sh_s.at[u, 1], sh_r.at[u, 1], behind, tp)
        tick, relay = u // 2, u % 2
        if relay == 0:
            copy = pltpu.make_async_copy(result, out.at[0, tick, 0], out_sem.at[tick * 2 + which])
            copy.start()
            outs.append(copy)

    def turn_out(u, result, out, which):
        tick = u // 2
        k = tick * 2 + which
        returned.append(send(result, out.at[1, tick, 0], ro_s.at[k], ro_r.at[k], mirror, tp))

    def ox(u):
        turn_out(u, yb.at[u], acts_out, 0)

    def oc(u):
        turn_out(u, gb.at[u], grads_out, 1)

    taken = set()

    def fresh(i):
        if i not in taken:
            taken.add(i)
            loads[i].wait()

    def take_x(u):
        shifted[u, 0].wait_recv()
        fresh(4)

        @pl.when(sec == 0)
        def _():
            x[u + 2, own] = fa[u]

    def take_c(u):
        shifted[u, 1].wait_recv()
        fresh(5)

        @pl.when(sec == n_sec - 1)
        def _():
            c[u + 2] = fc[u]

    reduced = {}

    def part(u, which):
        return contract_last(c[u], w[block(which), :])

    def rs_send(u, i, value, to_tp):
        ps[u, i] = value.astype(BF16)
        reduced.setdefault(u, {})[i] = send(
            ps.at[u, i], pr.at[u, i], rs_s.at[u, i], rs_r.at[u, i], sec, to_tp
        )

    def got(u, i):
        reduced[u][i].wait_recv()
        return pr[u, i].astype(F32)

    def r0a(u):
        rs_send(u, 0, part(u, tt), pp)

    def r0b(u):
        rs_send(u, 1, part(u, to), mm)

    def r1a(u):
        rs_send(u, 2, part(u, po), pp)

    def r1b(u):
        rs_send(u, 3, part(u, mm), mm)

    def r2a(u):
        rs_send(u, 4, part(u, pp) + got(u, 0), pp)

    def r2b(u):
        rs_send(u, 5, part(u, mo) + got(u, 1), mm)

    def r3(u):
        rs_send(u, 6, part(u, across) + got(u, 5) + got(u, 2), across)

    summed = {}
    row8 = lax.broadcasted_iota(jnp.int32, (8, 128), 0)

    def three_terms(value):
        first = value.astype(BF16).astype(F32)
        second = (value - first).astype(BF16).astype(F32)
        third = value - first - second
        return jnp.where(row8 == 0, first, jnp.where(row8 == 1, second, jnp.where(row8 == 2, third, 0.0)))

    def split_sum(value):
        ones = jnp.ones((16, cols), BF16)
        high = value.astype(BF16)
        low = (value - high.astype(F32)).astype(BF16)
        return (contract_last(ones, high) + contract_last(ones, low))[0:8]

    def r4(u):
        floats = s[u].astype(F32)
        at = block(own)
        pair = jnp.concatenate([left[0:rank, at] * left[rank:2 * rank, at], right[0:rank, 0:cols]], axis=0).astype(BF16)
        sm[u, own, 0:16] = jnp.concatenate(
            [contract_last(pair, c[u])[8:16], contract_last(pair, s[u])[0:8]], axis=0
        ).astype(BF16)
        squares = three_terms(split_sum(floats * floats))
        total = part(u, own) + got(u, 4) + got(u, 3) + got(u, 6)
        acc_g[u] = total
        crossed = three_terms(split_sum(s[u].astype(F32) * total))
        sm[u, own, 16:32] = jnp.concatenate([squares, crossed], axis=0).astype(BF16)
        mine = sm.at[u, own]
        summed[u] = [
            send(mine, mine, sm_s.at[u, k - 1], sm_r.at[u, k - 1], sec, (tp + k) % n_tp)
            for k in range(1, n_tp)
        ]

    def r5(u):
        for copy in summed[u]:
            copy.wait_recv()
        total = jnp.sum(sm[u].astype(F32), axis=0)
        low, latent = total[0:8], total[8:16]
        inv = lax.rsqrt(jnp.sum(total[16:24], axis=0, keepdims=True) / width + EPS)
        factor = inv * inv * inv * jnp.sum(total[24:32], axis=0, keepdims=True) / width
        turned = jnp.transpose(jnp.where(row8 < 4, inv, factor))
        inv_col, factor_col = turned[:, 0:1], turned[:, 4:5]
        floats = s[u].astype(F32)
        gb[u] = (c[u].astype(F32) + inv_col * acc_g[u] - factor_col * floats).astype(BF16)
        finish(u, gb.at[u], grads_out, 1)
        zeros = jnp.zeros_like(low)
        low16 = jnp.concatenate([low * inv, zeros], axis=0).astype(BF16)
        latent16 = jnp.concatenate([latent * inv, zeros], axis=0).astype(BF16)
        ga_acc[...] += jnp.dot(low16, s[u], preferred_element_type=F32)[0:8]
        gb_acc[...] += jnp.dot(latent16, c[u], preferred_element_type=F32)[0:8]

    def begin_c(u):
        if u == D0:
            loads[1].wait()
        elif u == U0:
            turned_in["c"].wait_recv()
        else:
            take_c(u - 2)
        r0a(u)

    def begin_x(u):
        if u == D0:
            loads[0].wait()
        elif u == U0:
            turned_in["x"].wait_recv()
        else:
            take_x(u - 2)
        ag0(u)

    def begin_s(u):
        if u in (U0, U1):
            turned_in[u].wait_recv()
        else:
            loads[2 + u // 2].wait()
        r4(u)

    shares = []

    def share_a():
        gar[own] = ga_acc[...] * left[rank:2 * rank, block(own)]
        mine = gar.at[own]
        for k in range(1, n_tp):
            shares.append(send(mine, mine, ga_s.at[k - 1], ga_r.at[k - 1], sec, (tp + k) % n_tp))
        grad_b[0] = gb_acc[...]

    steps = {
        "build": build, "rev_c": rev_c, "rev_x": rev_x, "send_s": rev_s,
        "ag0": begin_x, "ag1": ag1, "ag2a": ag2a, "ag2b": ag2b, "ag3": ag3,
        "f0": f0, "f1": f1, "f2": f2, "f3": f3,
        "r0a": begin_c, "r0b": r0b, "r1a": r1a, "r1b": r1b, "r2a": r2a, "r2b": r2b, "r3": r3,
        "r4": begin_s, "r5": r5, "ox": ox, "oc": oc,
    }
    last = [which for which in SCHEDULE if which[0] == "r5"][-1]
    for step, u in SCHEDULE:
        steps[step](u)
        if (step, u) == last:
            share_a()
    for copy in shares:
        copy.wait_recv()
    for k in range(n_tp):
        grad_a[0, :, k * cols:(k + 1) * cols] = gar[k]
    for copy in outs:
        copy.wait()
    for copy in returned:
        copy.wait_recv()
    for copy in sends:
        copy.wait_send()


def settle(acts, grads, sum_a, sum_b, acts_out, grads_out, grad_a, grad_b, held, sem_in, sem_out):
    pairs = [(src, dst, r, k) for r in range(2) for k in range(acts.shape[1]) for src, dst in ((acts, acts_out), (grads, grads_out))]
    takes = [pltpu.make_async_copy(src.at[r, k, 0], held.at[i], sem_in.at[i]) for i, (src, dst, r, k) in enumerate(pairs)]
    gives = [pltpu.make_async_copy(held.at[i], dst.at[r, k, 0], sem_out.at[i]) for i, (src, dst, r, k) in enumerate(pairs)]
    for take in takes:
        take.start()
    grad_a[...] = sum_a[...].astype(BF16)
    grad_b[...] = sum_b[...].astype(BF16)
    for take, give in zip(takes, gives):
        take.wait()
        give.start()
    for give in gives:
        give.wait()


def body(acts_in, cots_in, stash, fresh_acts, fresh_cots, gains, weights, adapter_a, adapter_b):
    rows, cols = acts_in.shape[2], acts_in.shape[3]
    ticks = stash.shape[1]
    rank, width = adapter_a.shape[1], adapter_a.shape[2]
    n_tp = width // cols
    units = 2 * ticks
    hbm, vmem = pl.BlockSpec(memory_space=pl.ANY), pl.BlockSpec(memory_space=pltpu.VMEM)
    dma = pltpu.SemaphoreType.DMA
    tile = (rows, cols)
    out = jax.ShapeDtypeStruct((2, ticks, 1, rows, cols), BF16)
    results = pl.pallas_call(
        kernel,
        name="relays",
        out_shape=(
            out,
            out,
            jax.ShapeDtypeStruct((1, rank, width), F32),
            jax.ShapeDtypeStruct((1, rank, cols), F32),
        ),
        in_specs=[hbm, hbm, hbm, hbm, hbm, vmem, hbm, vmem, vmem],
        out_specs=(hbm, hbm, vmem, vmem),
        scratch_shapes=[
            pltpu.VMEM((width, cols), BF16),
            pltpu.VMEM((units, n_tp) + tile, BF16),
            pltpu.VMEM((units,) + tile, BF16),
            pltpu.VMEM((units,) + tile, BF16),
            pltpu.VMEM((2,) + tile, BF16),
            pltpu.VMEM((2,) + tile, BF16),
            pltpu.VMEM((units, 7) + tile, BF16),
            pltpu.VMEM((units, 7) + tile, BF16),
            pltpu.VMEM((units,) + tile, BF16),
            pltpu.VMEM((units,) + tile, BF16),
            pltpu.VMEM((units, n_tp, 32, rows), BF16),
            pltpu.VMEM((n_tp, rank, cols), F32),
            pltpu.VMEM((units,) + tile, F32),
            pltpu.VMEM((units,) + tile, F32),
            pltpu.VMEM((units, rows, 128), F32),
            pltpu.VMEM((2 * rank, width), F32),
            pltpu.VMEM((2 * rank, cols + 128), F32),
            pltpu.VMEM((rank, cols), F32),
            pltpu.VMEM((rank, cols), F32),
            dma((n_tp,)),
            dma((6,)),
            dma((4,)),
            dma((units, 8)),
            dma((units, 8)),
            dma((units, 7)),
            dma((units, 7)),
            dma((units, 7)),
            dma((units, 7)),
            dma((2, 2)),
            dma((2, 2)),
            dma((4,)),
            dma((4,)),
            dma((4,)),
            dma((4,)),
            dma((7,)),
            dma((7,)),
        ],
        compiler_params=pltpu.CompilerParams(
            collective_id=0, has_side_effects=True, vmem_limit_bytes=56 * 1024 * 1024
        ),
    )(acts_in, cots_in, stash, fresh_acts, fresh_cots, gains, weights, adapter_a, adapter_b)
    return pl.pallas_call(
        settle,
        name="settle",
        out_shape=(
            out,
            out,
            jax.ShapeDtypeStruct((1, rank, width), BF16),
            jax.ShapeDtypeStruct((1, rank, cols), BF16),
        ),
        in_specs=[hbm, hbm, vmem, vmem],
        out_specs=(hbm, hbm, vmem, vmem),
        scratch_shapes=[pltpu.VMEM((4 * ticks,) + tile, BF16), dma((4 * ticks,)), dma((4 * ticks,))],
    )(*results)


def solution(mesh):
    in_specs = (
        P(None, "section", None, "tp"),
        P(None, "section", None, "tp"),
        P(None, None, "section", None, "tp"),
        P(None, None, None, "tp"),
        P(None, None, None, "tp"),
        P("section", None),
        P("section", None, "tp"),
        P("section", None, None),
        P("section", None, "tp"),
    )
    out_specs = (
        P(None, None, "section", None, "tp"),
        P(None, None, "section", None, "tp"),
        P("section", None, None),
        P("section", None, "tp"),
    )
    return jax.shard_map(body, mesh=mesh, in_specs=in_specs, out_specs=out_specs, check_vma=False)
```

```python
import jax
import jax.numpy as jnp
from jax import lax
from jax.experimental import pallas as pl
from jax.experimental.pallas import tpu as pltpu
from jax.sharding import PartitionSpec as P

EPS = 1e-05
MESH = pl.DeviceIdType.MESH
F32 = jnp.float32
BF16 = jnp.bfloat16

D0, U0, D1, U1 = range(4)

SCHEDULE = (
    ("ag0", 0), ("rev_x", 1), ("build", 0), ("r0a", 0), ("build", 1), ("ag2b", 0), ("r0b", 0), ("build", 3),
    ("ag2a", 0), ("build", 2), ("ag0", 1), ("rev_c", 1), ("build", 5), ("r1a", 0), ("build", 4), ("r2b", 0),
    ("build", 7), ("r1b", 0), ("r2a", 0), ("build", 6), ("r0a", 1), ("r3", 0), ("r0b", 1), ("f0", 0),
    ("r4", 0), ("ag2b", 1), ("send_s", 1), ("ag3", 0), ("ag2a", 1), ("r1a", 1), ("r2b", 1), ("ag1", 1),
    ("f2", 0), ("f0", 1), ("r5", 0), ("ag3", 1), ("f2", 1), ("r2a", 1), ("r1b", 1), ("r3", 1),
    ("ag1", 0), ("r0a", 2), ("f1", 1), ("r0b", 2), ("r4", 1), ("f3", 1), ("r1b", 2), ("send_s", 3),
    ("r1a", 2), ("r5", 1), ("ag0", 3), ("ox", 1), ("r2b", 2), ("r0a", 3), ("ag2a", 3), ("oc", 1),
    ("r0b", 3), ("f1", 0), ("r1a", 3), ("f0", 3), ("ag2b", 3), ("r3", 2), ("r2b", 3), ("ag3", 3),
    ("ag1", 3), ("f3", 0), ("f2", 3), ("r2a", 3), ("r3", 3), ("r1b", 3), ("r2a", 2), ("f1", 3),
    ("f3", 3), ("ox", 3), ("r4", 3), ("ag0", 2), ("r4", 2), ("r5", 3), ("oc", 3), ("ag2b", 2),
    ("ag2a", 2), ("r5", 2), ("ag1", 2), ("ag3", 2), ("f0", 2), ("f2", 2), ("f1", 2), ("f3", 2),
)


def contract_last(left, right):
    return lax.dot_general(left, right, (((1,), (1,)), ((), ())), preferred_element_type=F32)


def contract_first(left, right):
    return lax.dot_general(left, right, (((0,), (0,)), ((), ())), preferred_element_type=F32)


def kernel(
    acts, cots, stash, fresh_acts, fresh_cots, gain, weights, lower, upper,
    acts_out, grads_out, grad_a, grad_b,
    w, x, c, s, fa, fc, ps, pr, yb, gb, sm, gar, acc, acc_g, sq, left, right, ga_acc, gb_acc,
    w_sem, in_sem, out_sem,
    ag_s, ag_r, rs_s, rs_r, sm_s, sm_r, sh_s, sh_r, ri_s, ri_r, ro_s, ro_r, ga_s, ga_r,
):
    sec, tp = lax.axis_index("section"), lax.axis_index("tp")
    n_sec, n_tp = lax.axis_size("section"), lax.axis_size("tp")
    cols = w.shape[1]
    width = n_tp * cols
    rank = lower.shape[1]
    nx = n_tp // 2
    xi, yi = tp // 2, tp % 2
    turn = 1 - 2 * yi
    xp, xm, x2 = (xi + turn + nx) % nx, (xi - turn + nx) % nx, (xi + 2) % nx
    yo = 1 - yi
    own, across = tp, xi * 2 + yo
    pp, po, mm, mo, tt, to = xp * 2 + yi, xp * 2 + yo, xm * 2 + yi, xm * 2 + yo, x2 * 2 + yi, x2 * 2 + yo
    ahead, behind, mirror = (sec + 1) % n_sec, (sec + n_sec - 1) % n_sec, n_sec - 1 - sec
    sends = []

    def send(src, dst, send_sem, recv_sem, to_sec, to_tp):
        copy = pltpu.make_async_remote_copy(
            src_ref=src, dst_ref=dst, send_sem=send_sem, recv_sem=recv_sem,
            device_id=(to_sec, to_tp), device_id_type=MESH,
        )
        copy.start()
        sends.append(copy)
        return copy

    def block(index):
        return pl.ds(pl.multiple_of(index * cols, cols), cols)

    order = (tt, to, po, mm, pp, mo, across, own)
    loads = [
        pltpu.make_async_copy(acts.at[0, 0], x.at[D0, own], in_sem.at[0]),
        pltpu.make_async_copy(cots.at[0, 0], c.at[D0], in_sem.at[1]),
    ]
    w_loads = [
        pltpu.make_async_copy(weights.at[0, block(which)], w.at[block(which)], w_sem.at[i])
        for i, which in enumerate(order)
    ]
    loads += [
        pltpu.make_async_copy(stash.at[0, 0, 0], s.at[D0], in_sem.at[2]),
        pltpu.make_async_copy(stash.at[0, 1, 0], s.at[D1], in_sem.at[3]),
        pltpu.make_async_copy(fresh_acts.at[:, 0], fa, in_sem.at[4]),
        pltpu.make_async_copy(fresh_cots.at[:, 0], fc, in_sem.at[5]),
    ]
    for copy in loads[:2] + w_loads + loads[2:]:
        copy.start()

    barrier = pltpu.get_barrier_semaphore()
    peers = [(sec, (tp + k) % n_tp) for k in range(1, n_tp)]
    peers += [(mirror, tp), (ahead, tp), (behind, tp)]
    for peer in peers:
        pl.semaphore_signal(barrier, inc=1, device_id=peer, device_id_type=MESH)
    pl.semaphore_wait(barrier, len(peers))

    turned_in = {}

    def rev_c(u):
        turned_in["c"] = send(cots.at[1, 0], c.at[u], ri_s.at[0], ri_r.at[0], mirror, tp)

    def rev_x(u):
        turned_in["x"] = send(acts.at[1, 0], x.at[u, own], ri_s.at[1], ri_r.at[1], mirror, tp)

    def rev_s(u):
        tick = u // 2
        turned_in[u] = send(stash.at[1, tick, 0], s.at[u], ri_s.at[2 + tick], ri_r.at[2 + tick], mirror, tp)

    left[0:rank] = lower[0].astype(F32)
    left[rank:2 * rank] = jnp.broadcast_to(gain[...].astype(F32), (rank, width))
    row = lax.broadcasted_iota(jnp.int32, (rank, 128), 0)
    right[0:rank, 0:cols] = upper[0].astype(F32)
    right[rank:2 * rank, 0:cols] = jnp.zeros((rank, cols), F32)
    right[0:rank, cols:cols + 128] = jnp.zeros((rank, 128), F32)
    right[rank:2 * rank, cols:cols + 128] = jnp.where(row == 0, 1.0, 0.0).astype(F32)
    ga_acc[...] = jnp.zeros_like(ga_acc)
    gb_acc[...] = jnp.zeros_like(gb_acc)

    def build(i):
        w_loads[i].wait()
        base = order[i] * cols

        def step(j, carry):
            at = pl.ds(pl.multiple_of(base + j * 128, 128), 128)
            both = contract_first(left[:, at].astype(BF16), right[...].astype(BF16))
            scale = both[:, cols:cols + 128]
            for k in range(cols // 128):
                lanes = slice(k * 128, (k + 1) * 128)
                w[at, lanes] = ((w[at, lanes].astype(F32) + both[:, lanes]) * scale).astype(BF16)
            return carry

        lax.fori_loop(0, cols // 128, step, 0)

    gathered, here = {}, set()

    def arrive(u, i):
        if (u, i) not in here:
            here.add((u, i))
            gathered[u][i].wait_recv()

    def ag0(u):
        mine = x.at[u, own]
        gathered[u] = {
            i: send(mine, mine, ag_s.at[u, i], ag_r.at[u, i], sec, to_tp)
            for i, to_tp in enumerate((across, pp, mm))
        }

    def ag1(u):
        arrive(u, 0)
        part = x.at[u, across]
        for i, to_tp in ((3, pp), (4, mm)):
            gathered[u][i] = send(part, part, ag_s.at[u, i], ag_r.at[u, i], sec, to_tp)

    def ag2(u, k, wait, which, to_tp):
        half = x.shape[2] // 2
        arrive(u, wait)
        piece = x.at[u, which, pl.ds(k * half, half)]
        gathered[u][5 + k] = send(piece, piece, ag_s.at[u, 5 + k], ag_r.at[u, 5 + k], sec, to_tp)

    def ag2a(u):
        ag2(u, 0, 1, mm, pp)

    def ag2b(u):
        ag2(u, 1, 2, pp, mm)

    def ag3(u):
        arrive(u, 5)
        arrive(u, 6)
        far = x.at[u, tt]
        gathered[u][7] = send(far, far, ag_s.at[u, 7], ag_r.at[u, 7], sec, across)

    def fwd(u, which, first=False):
        rows = x[u, which]
        floats = rows.astype(F32)
        squares = floats * floats
        total = squares[:, 0:128]
        for k in range(1, cols // 128):
            total = total + squares[:, k * 128:(k + 1) * 128]
        product = jnp.dot(rows, w[block(which), :], preferred_element_type=F32)
        if first:
            sq[u] = total
            acc[u] = product
        else:
            sq[u] += total
            acc[u] += product

    def f0(u):
        fwd(u, own, True)
        for i, which in ((1, mm), (2, pp), (0, across)):
            arrive(u, i)
            fwd(u, which)

    def f1(u):
        for i, which in ((3, mo), (4, po)):
            arrive(u, i)
            fwd(u, which)

    def f2(u):
        arrive(u, 5)
        arrive(u, 6)
        fwd(u, tt)

    def f3(u):
        arrive(u, 7)
        fwd(u, to)
        inv = lax.rsqrt(jnp.sum(sq[u], axis=1, keepdims=True) / width + EPS)
        yb[u] = (x[u, own].astype(F32) + inv * acc[u]).astype(BF16)
        finish(u, yb.at[u], acts_out, 0)

    shifted, outs, returned = {}, [], []

    def finish(u, result, out, which):
        if u < 2:
            target = c.at[u + 2] if which else x.at[u + 2, own]

            def shift():
                return pltpu.make_async_remote_copy(
                    src_ref=result, dst_ref=target, send_sem=sh_s.at[u, which], recv_sem=sh_r.at[u, which],
                    device_id=(behind if which else ahead, tp), device_id_type=MESH,
                )

            shifted[u, which] = shift

            @pl.when(sec != (0 if which else n_sec - 1))
            def _():
                shift().start()

        tick, relay = u // 2, u % 2
        if relay == 0:
            copy = pltpu.make_async_copy(result, out.at[0, tick, 0], out_sem.at[tick * 2 + which])
            copy.start()
            outs.append(copy)

    def turn_out(u, result, out, which):
        tick = u // 2
        k = tick * 2 + which
        returned.append(send(result, out.at[1, tick, 0], ro_s.at[k], ro_r.at[k], mirror, tp))

    def ox(u):
        turn_out(u, yb.at[u], acts_out, 0)

    def oc(u):
        turn_out(u, gb.at[u], grads_out, 1)

    taken = set()

    def fresh(i):
        if i not in taken:
            taken.add(i)
            loads[i].wait()

    def take_x(u):
        fresh(4)

        @pl.when(sec != 0)
        def _():
            shifted[u, 0]().wait_recv()

        @pl.when(sec == 0)
        def _():
            x[u + 2, own] = fa[u]

    def take_c(u):
        fresh(5)

        @pl.when(sec != n_sec - 1)
        def _():
            shifted[u, 1]().wait_recv()

        @pl.when(sec == n_sec - 1)
        def _():
            c[u + 2] = fc[u]

    reduced = {}

    def part(u, which):
        return contract_last(c[u], w[block(which), :])

    def rs_send(u, i, value, to_tp):
        ps[u, i] = value.astype(BF16)
        reduced.setdefault(u, {})[i] = send(
            ps.at[u, i], pr.at[u, i], rs_s.at[u, i], rs_r.at[u, i], sec, to_tp
        )

    def got(u, i):
        reduced[u][i].wait_recv()
        return pr[u, i].astype(F32)

    def r0a(u):
        rs_send(u, 0, part(u, tt), pp)

    def r0b(u):
        rs_send(u, 1, part(u, to), mm)

    def r1a(u):
        rs_send(u, 2, part(u, po), pp)

    def r1b(u):
        rs_send(u, 3, part(u, mm), mm)

    def r2a(u):
        rs_send(u, 4, part(u, pp) + got(u, 0), pp)

    def r2b(u):
        rs_send(u, 5, part(u, mo) + got(u, 1), mm)

    def r3(u):
        rs_send(u, 6, part(u, across) + got(u, 5) + got(u, 2), across)

    summed = {}
    row8 = lax.broadcasted_iota(jnp.int32, (8, 128), 0)

    def three_terms(value):
        first = value.astype(BF16).astype(F32)
        second = (value - first).astype(BF16).astype(F32)
        third = value - first - second
        return jnp.where(row8 == 0, first, jnp.where(row8 == 1, second, jnp.where(row8 == 2, third, 0.0)))

    def split_sum(value):
        ones = jnp.ones((16, cols), BF16)
        high = value.astype(BF16)
        low = (value - high.astype(F32)).astype(BF16)
        return (contract_last(ones, high) + contract_last(ones, low))[0:8]

    def r4(u):
        floats = s[u].astype(F32)
        at = block(own)
        pair = jnp.concatenate([left[0:rank, at] * left[rank:2 * rank, at], right[0:rank, 0:cols]], axis=0).astype(BF16)
        sm[u, own, 0:16] = jnp.concatenate(
            [contract_last(pair, c[u])[8:16], contract_last(pair, s[u])[0:8]], axis=0
        ).astype(BF16)
        squares = three_terms(split_sum(floats * floats))
        total = part(u, own) + got(u, 4) + got(u, 3) + got(u, 6)
        acc_g[u] = total
        crossed = three_terms(split_sum(s[u].astype(F32) * total))
        sm[u, own, 16:32] = jnp.concatenate([squares, crossed], axis=0).astype(BF16)
        mine = sm.at[u, own]
        summed[u] = [
            send(mine, mine, sm_s.at[u, k - 1], sm_r.at[u, k - 1], sec, (tp + k) % n_tp)
            for k in range(1, n_tp)
        ]

    def r5(u):
        for copy in summed[u]:
            copy.wait_recv()
        total = jnp.sum(sm[u].astype(F32), axis=0)
        low, latent = total[0:8], total[8:16]
        inv = lax.rsqrt(jnp.sum(total[16:24], axis=0, keepdims=True) / width + EPS)
        factor = inv * inv * inv * jnp.sum(total[24:32], axis=0, keepdims=True) / width
        turned = jnp.transpose(jnp.where(row8 < 4, inv, factor))
        inv_col, factor_col = turned[:, 0:1], turned[:, 4:5]
        floats = s[u].astype(F32)
        gb[u] = (c[u].astype(F32) + inv_col * acc_g[u] - factor_col * floats).astype(BF16)
        finish(u, gb.at[u], grads_out, 1)
        zeros = jnp.zeros_like(low)
        low16 = jnp.concatenate([low * inv, zeros], axis=0).astype(BF16)
        latent16 = jnp.concatenate([latent * inv, zeros], axis=0).astype(BF16)
        ga_acc[...] += jnp.dot(low16, s[u], preferred_element_type=F32)[0:8]
        gb_acc[...] += jnp.dot(latent16, c[u], preferred_element_type=F32)[0:8]

    def begin_c(u):
        if u == D0:
            loads[1].wait()
        elif u == U0:
            turned_in["c"].wait_recv()
        else:
            take_c(u - 2)
        r0a(u)

    def begin_x(u):
        if u == D0:
            loads[0].wait()
        elif u == U0:
            turned_in["x"].wait_recv()
        else:
            take_x(u - 2)
        ag0(u)

    def begin_s(u):
        if u in (U0, U1):
            turned_in[u].wait_recv()
        else:
            loads[2 + u // 2].wait()
        r4(u)

    shares = []

    def share_a():
        gar[own] = ga_acc[...] * left[rank:2 * rank, block(own)]
        mine = gar.at[own]
        for k in range(1, n_tp):
            shares.append(send(mine, mine, ga_s.at[k - 1], ga_r.at[k - 1], sec, (tp + k) % n_tp))
        grad_b[0] = gb_acc[...]

    steps = {
        "build": build, "rev_c": rev_c, "rev_x": rev_x, "send_s": rev_s,
        "ag0": begin_x, "ag1": ag1, "ag2a": ag2a, "ag2b": ag2b, "ag3": ag3,
        "f0": f0, "f1": f1, "f2": f2, "f3": f3,
        "r0a": begin_c, "r0b": r0b, "r1a": r1a, "r1b": r1b, "r2a": r2a, "r2b": r2b, "r3": r3,
        "r4": begin_s, "r5": r5, "ox": ox, "oc": oc,
    }
    last = [which for which in SCHEDULE if which[0] == "r5"][-1]
    for step, u in SCHEDULE:
        steps[step](u)
        if (step, u) == last:
            share_a()
    for copy in shares:
        copy.wait_recv()
    for k in range(n_tp):
        grad_a[0, :, k * cols:(k + 1) * cols] = gar[k]
    for copy in outs:
        copy.wait()
    for copy in returned:
        copy.wait_recv()
    for copy in sends:
        copy.wait_send()
    for which, final in ((0, n_sec - 1), (1, 0)):

        @pl.when(sec != final)
        def _():
            for u in (D0, U0):
                shifted[u, which]().wait_send()


def settle(acts, grads, sum_a, sum_b, acts_out, grads_out, grad_a, grad_b, held, sem_in, sem_out):
    pairs = [(src, dst, r, k) for r in range(2) for k in range(acts.shape[1]) for src, dst in ((acts, acts_out), (grads, grads_out))]
    takes = [pltpu.make_async_copy(src.at[r, k, 0], held.at[i], sem_in.at[i]) for i, (src, dst, r, k) in enumerate(pairs)]
    gives = [pltpu.make_async_copy(held.at[i], dst.at[r, k, 0], sem_out.at[i]) for i, (src, dst, r, k) in enumerate(pairs)]
    for take in takes:
        take.start()
    grad_a[...] = sum_a[...].astype(BF16)
    grad_b[...] = sum_b[...].astype(BF16)
    for take, give in zip(takes, gives):
        take.wait()
        give.start()
    for give in gives:
        give.wait()


def body(acts_in, cots_in, stash, fresh_acts, fresh_cots, gains, weights, adapter_a, adapter_b):
    rows, cols = acts_in.shape[2], acts_in.shape[3]
    ticks = stash.shape[1]
    rank, width = adapter_a.shape[1], adapter_a.shape[2]
    n_tp = width // cols
    units = 2 * ticks
    hbm, vmem = pl.BlockSpec(memory_space=pl.ANY), pl.BlockSpec(memory_space=pltpu.VMEM)
    dma = pltpu.SemaphoreType.DMA
    tile = (rows, cols)
    out = jax.ShapeDtypeStruct((2, ticks, 1, rows, cols), BF16)
    results = pl.pallas_call(
        kernel,
        name="relays",
        out_shape=(
            out,
            out,
            jax.ShapeDtypeStruct((1, rank, width), F32),
            jax.ShapeDtypeStruct((1, rank, cols), F32),
        ),
        in_specs=[hbm, hbm, hbm, hbm, hbm, vmem, hbm, vmem, vmem],
        out_specs=(hbm, hbm, vmem, vmem),
        scratch_shapes=[
            pltpu.VMEM((width, cols), BF16),
            pltpu.VMEM((units, n_tp) + tile, BF16),
            pltpu.VMEM((units,) + tile, BF16),
            pltpu.VMEM((units,) + tile, BF16),
            pltpu.VMEM((2,) + tile, BF16),
            pltpu.VMEM((2,) + tile, BF16),
            pltpu.VMEM((units, 7) + tile, BF16),
            pltpu.VMEM((units, 7) + tile, BF16),
            pltpu.VMEM((units,) + tile, BF16),
            pltpu.VMEM((units,) + tile, BF16),
            pltpu.VMEM((units, n_tp, 32, rows), BF16),
            pltpu.VMEM((n_tp, rank, cols), F32),
            pltpu.VMEM((units,) + tile, F32),
            pltpu.VMEM((units,) + tile, F32),
            pltpu.VMEM((units, rows, 128), F32),
            pltpu.VMEM((2 * rank, width), F32),
            pltpu.VMEM((2 * rank, cols + 128), F32),
            pltpu.VMEM((rank, cols), F32),
            pltpu.VMEM((rank, cols), F32),
            dma((n_tp,)),
            dma((6,)),
            dma((4,)),
            dma((units, 8)),
            dma((units, 8)),
            dma((units, 7)),
            dma((units, 7)),
            dma((units, 7)),
            dma((units, 7)),
            dma((2, 2)),
            dma((2, 2)),
            dma((4,)),
            dma((4,)),
            dma((4,)),
            dma((4,)),
            dma((7,)),
            dma((7,)),
        ],
        compiler_params=pltpu.CompilerParams(
            collective_id=0, has_side_effects=True, vmem_limit_bytes=56 * 1024 * 1024
        ),
    )(acts_in, cots_in, stash, fresh_acts, fresh_cots, gains, weights, adapter_a, adapter_b)
    return pl.pallas_call(
        settle,
        name="settle",
        out_shape=(
            out,
            out,
            jax.ShapeDtypeStruct((1, rank, width), BF16),
            jax.ShapeDtypeStruct((1, rank, cols), BF16),
        ),
        in_specs=[hbm, hbm, vmem, vmem],
        out_specs=(hbm, hbm, vmem, vmem),
        scratch_shapes=[pltpu.VMEM((4 * ticks,) + tile, BF16), dma((4 * ticks,)), dma((4 * ticks,))],
    )(*results)


def solution(mesh):
    in_specs = (
        P(None, "section", None, "tp"),
        P(None, "section", None, "tp"),
        P(None, None, "section", None, "tp"),
        P(None, None, None, "tp"),
        P(None, None, None, "tp"),
        P("section", None),
        P("section", None, "tp"),
        P("section", None, None),
        P("section", None, "tp"),
    )
    out_specs = (
        P(None, None, "section", None, "tp"),
        P(None, None, "section", None, "tp"),
        P("section", None, None),
        P("section", None, "tp"),
    )
    return jax.shard_map(body, mesh=mesh, in_specs=in_specs, out_specs=out_specs, check_vma=False)
```
